256 devices in a mesh: outer: 32 (over z_hi, y, core), inner: 8 (over x, z_lo).
Axes of the slice: x: 4, y: 4, z: 8 (z_hi: 4, z_lo: 2; z = z_hi * 2 + z_lo), core: 2. Of those that a mesh axis runs over, the one named last changes fastest.
Arguments:
- tokens: bfloat16 [512, 512, 1024], P('outer', 'inner'), may hold values from -6 to 6
- gate: bfloat16 [512, 512, 1024], P('outer', 'inner'), may hold values from 0.25 to 2
- upstream: bfloat16 [512, 512, 1024], P('outer', 'inner'), may hold values from -6 to 6
- first_factor: bfloat16 [8, 512, 512], P('inner'), may hold values from -0.25 to 0.25
- second_factor: bfloat16 [8, 512, 512], P('inner'), may hold values from -0.25 to 0.25
Outputs:
- token_grad: bfloat16 [512, 512, 1024], P('outer', 'inner')
- first_grad: float32 [8, 512, 512], P('inner', 'outer')
- second_grad: float32 [8, 512, 512], P('inner', 'outer')
The draws below stay inside these ranges and needn't reach their ends.
All inputs are finite; a program needn't handle non-finite values.
Results may differ from the reference program's by a relative error of at most 0.0057.
Values may be sent and summed in bfloat16 or wider, within the bound.
No kernel may reach another device: no remote copies, remote signals or barrier semaphores. Data moves between devices by JAX's collectives and lax.ppermute only.
A program may use at most 64 MiB of HBM per device.

```python
import jax
import jax.numpy as jnp
from jax import lax

ROWS = 512
COLS = 512
D = 1024
SLAB = 128
S = 8


def shard_levels(key, extent, cuts, smallest, largest):
    factor_of = 1.0
    for dim, parts in cuts:
        steps = jax.random.uniform(jax.random.fold_in(jax.random.fold_in(key, 6), dim), (parts,), jnp.float32, smallest / len(cuts), largest / len(cuts))
        factor_of = factor_of * jnp.repeat(jnp.exp(steps), extent[dim] // parts).reshape((-1,) + (1,) * (len(extent) - 1 - dim))
    return factor_of


def centred(rng, extent, width, bound, pieces=(), held_as=jnp.bfloat16):
    entries = width * jax.random.normal(rng, extent, jnp.float32)
    if pieces:
        entries = entries * shard_levels(rng, extent, pieces, -0.22, 0.18)
    return jnp.clip(entries, -bound, bound).astype(held_as)


def setup_inputs(seed: int = 0) -> dict:
    key_of = jax.random.split(jax.random.key(seed), 6)
    tokens = centred(key_of[0], (ROWS, COLS, D), 1.0, 6.0, ((0, 32), (1, 8)))
    gate = jnp.clip(0.25 + 1.75 * jax.random.uniform(key_of[1], (ROWS, COLS, D), jnp.float32) ** shard_levels(key_of[1], (ROWS, COLS, D), ((0, 32), (1, 8)), -0.2, 0.2), 0.25, 2.0).astype(jnp.bfloat16)
    upstream = centred(key_of[2], (ROWS, COLS, D), 1.0, 6.0, ((0, 32), (1, 8)))
    first_factor = centred(key_of[3], (S, COLS, COLS), COLS ** -0.5, 0.25, ((0, 8),))
    second_factor = centred(key_of[4], (S, ROWS, ROWS), ROWS ** -0.5, 0.25, ((0, 8),))
    return {"tokens": tokens, "gate": gate, "upstream": upstream, "first_factor": first_factor, "second_factor": second_factor}


def slab_backward(operands):
    tok_slab, gate_slab, up_slab, first_block, second_block = operands
    first_f = first_block.astype(jnp.float32)
    second_f = second_block.astype(jnp.float32)
    gated_grad = (gate_slab.astype(jnp.float32) * up_slab.astype(jnp.float32)).astype(jnp.bfloat16)
    mixed = jnp.einsum("pq,rqk->rpk", first_f, tok_slab.astype(jnp.float32)).astype(jnp.bfloat16)
    second_grad = jnp.einsum("qck,rck->qr", gated_grad.astype(jnp.float32), mixed.astype(jnp.float32))
    second_grad = second_grad * (COLS ** -0.5) * (SLAB ** -0.5)
    mixed_grad = jnp.einsum("qr,qck->rck", second_f, gated_grad.astype(jnp.float32)).astype(jnp.bfloat16)
    first_grad = jnp.einsum("rpk,rck->pc", mixed_grad.astype(jnp.float32), tok_slab.astype(jnp.float32))
    first_grad = first_grad * (ROWS ** -0.5) * (SLAB ** -0.5)
    token_grad = jnp.einsum("pc,rpk->rck", first_f, mixed_grad.astype(jnp.float32)).astype(jnp.bfloat16)
    return token_grad, first_grad, second_grad


def to_slabs(array):
    return jnp.moveaxis(array.reshape(ROWS, COLS, S, SLAB), 2, 0)


def reference(tokens, gate, upstream, first_factor, second_factor):
    token_slabs, first_grad, second_grad = lax.map(
        slab_backward, (to_slabs(tokens), to_slabs(gate), to_slabs(upstream), first_factor, second_factor))
    token_grad = jnp.moveaxis(token_slabs, 0, 2).reshape(ROWS, COLS, D)
    return token_grad, first_grad, second_grad
```

```python
import functools

import jax
import jax.numpy as jnp
from jax import lax
from jax.experimental import pallas as pl
from jax.experimental.pallas import tpu as pltpu
from jax.sharding import Mesh, PartitionSpec as P

ROWS = 512
COLS = 512
SLAB = 128
BF = jnp.bfloat16
F32 = jnp.float32
ZYC = ("zh", "y", "core", "zl")
PLANE = ("y", "core", "x")
PARAMS = pltpu.CompilerParams(vmem_limit_bytes=48 * 1024 * 1024)
VM = pl.BlockSpec(memory_space=pltpu.VMEM)
SM = pl.BlockSpec(memory_space=pltpu.SMEM)


def call(kernel, outs, scratch=(), n_in=1, flops=0, moved=4 << 20):
    return pl.pallas_call(
        kernel,
        out_shape=outs,
        in_specs=[SM] + [VM] * n_in,
        out_specs=jax.tree.map(lambda _: VM, outs),
        scratch_shapes=list(scratch),
        compiler_params=PARAMS,
        cost_estimate=pl.CostEstimate(flops=flops, bytes_accessed=moved, transcendentals=0),
    )


def shape(*dims, dtype=BF):
    return jax.ShapeDtypeStruct(dims, dtype)


def gate_kernel(gate, up, out):
    prod = gate[...].astype(F32) * up[...].astype(F32)
    out[0, :, 0] = jnp.swapaxes(prod, 0, 1).astype(BF).reshape(8, 8, 16, SLAB)


def gate_call(gate, up):
    return pl.pallas_call(
        gate_kernel,
        grid=(8,),
        out_shape=shape(4, 8, 2, 8, 16, SLAB),
        in_specs=[pl.BlockSpec((16, 64, SLAB), lambda s: (0, 0, s))] * 2,
        out_specs=pl.BlockSpec((1, 8, 1, 8, 16, SLAB), lambda s: (s // 2, 0, s % 2, 0, 0, 0)),
        compiler_params=PARAMS,
        cost_estimate=pl.CostEstimate(flops=1 << 20, bytes_accessed=6 << 20, transcendentals=0),
    )(gate, up)


def factor_kernel(pos, *refs):
    yc = pos[2]
    f1, f2t, f1tp, full = refs[8:]
    for s in range(8):
        rows = pl.ds(pl.multiple_of(lax.rem(yc + 8 - s, 8) * 64, 64), 64)
        full[:, rows, :] = refs[s][...].astype(F32)
    f1[...] = full[0].astype(BF)
    f2t[...] = full[1].T.astype(BF)
    ordered = jnp.concatenate(
        [full[0, k * 64 + c * 8 : k * 64 + c * 8 + 8, :] for c in range(8) for k in range(8)], axis=0
    )
    f1tp[...] = ordered.T.astype(BF)


def second_apply_kernel(pos, f2t, g, out, flat, swap):
    for k in range(16):
        flat[:, k * SLAB : (k + 1) * SLAB] = g[:, :, k // 8, k % 8].reshape(ROWS, SLAB)

    def body(zh, _):
        rows = pl.ds(pl.multiple_of(zh * 128, 128), 128)
        for k in range(0, 16, 2):
            part = jnp.dot(f2t[rows, :], flat[:, k * SLAB : (k + 2) * SLAB], preferred_element_type=F32)
            swap[pl.ds(k, 128, stride=16), :] = part[:, :SLAB]
            swap[pl.ds(k + 1, 128, stride=16), :] = part[:, SLAB:]
        for yc in range(8):
            tile = swap[yc * 256 : (yc + 1) * 256, :].astype(BF).reshape(4, 4, 16, SLAB)
            for x in range(4):
                out[yc, x, zh] = tile[x]
        return 0

    lax.fori_loop(0, 4, body, 0)


def first_apply_kernel(pos, f1tp, m, o0, o1, o2, o3):
    x = pos[0]
    for s, out in enumerate((o0, o1, o2, o3)):
        rows = pl.ds(pl.multiple_of(lax.rem(x + s, 4) * 128, 128), 128)
        left = f1tp[rows, :]
        for zh in range(4):
            for r in range(0, 4, 2):
                right = jnp.concatenate(
                    [m[:, :, zh, r].reshape(COLS, SLAB), m[:, :, zh, r + 1].reshape(COLS, SLAB)], axis=1
                )
                part = jnp.dot(left, right, preferred_element_type=F32).astype(BF)
                out[zh, r] = part[:, :SLAB].reshape(2, 64, SLAB)
                out[zh, r + 1] = part[:, SLAB:].reshape(2, 64, SLAB)


def token_cut_kernel(pos, x0, x1, x2, x3, *outs):
    x, z = pos[0], pos[1]
    for s, block in enumerate((x0, x1, x2, x3)):
        source = lax.rem(x + 4 - s, 4)
        for t, out in enumerate(outs):
            lanes = pl.ds(pl.multiple_of(lax.rem(z + t, 8) * SLAB, SLAB), SLAB)
            out[source] = block[:, :, lanes]


def grad_cut_kernel(pos, x0, x1, x2, x3, *outs):
    x, z = pos[0], pos[1]
    for s, block in enumerate((x0, x1, x2, x3)):
        source = lax.rem(x + 4 - s, 4)
        for t, out in enumerate(outs):
            owner = lax.rem(z + t, 8)
            for r in range(4):
                out[source, r] = block[owner // 2, r, lax.rem(owner, 2)]


def grad_join_kernel(pos, *refs):
    z = pos[1]
    out = refs[8]
    for t in range(8):
        lanes = pl.ds(pl.multiple_of(lax.rem(z + 8 - t, 8) * SLAB, SLAB), SLAB)
        out[:, :, lanes] = refs[t][...].reshape(16, 64, SLAB)


def mix_kernel(pos, f1, p0, p1, p2, p3, p4, p5, p6, p7, mixed, tokw, tok, swap):
    z = pos[1]
    for t, block in enumerate((p0, p1, p2, p3, p4, p5, p6, p7)):
        source = lax.rem(z + 8 - t, 8)
        for r in range(4):
            for x in range(4):
                tok[source // 2, r, x, lax.rem(source, 2)] = block[x, r]
    for k in range(16):
        tokw[:, k * SLAB : (k + 1) * SLAB] = tok[k // 4, k % 4].reshape(COLS, SLAB)

    def body(b, _):
        rows = pl.ds(pl.multiple_of(b * 128, 128), 128)
        for k in range(0, 16, 2):
            part = jnp.dot(f1[rows, :], tokw[:, k * SLAB : (k + 2) * SLAB], preferred_element_type=F32)
            swap[pl.ds(k, 128, stride=16), :] = part[:, :SLAB]
            swap[pl.ds(k + 1, 128, stride=16), :] = part[:, SLAB:]
        for zl in range(2):
            tile = swap[zl * 1024 : (zl + 1) * 1024, :].astype(BF).reshape(8, 8, 16, SLAB)
            for yc in range(8):
                mixed[yc, b, zl] = tile[yc]
        return 0

    lax.fori_loop(0, 4, body, 0)


def first_kernel(pos, m, tokw, first, mgw):
    for k in range(16):
        mgw[:, k * SLAB : (k + 1) * SLAB] = m[:, :, k // 4, k % 4].reshape(COLS, SLAB)
    for yc in range(8):
        left = mgw[yc * 64 : (yc + 1) * 64, :]
        part = lax.dot_general(left, tokw[...], (((1,), (1,)), ((), ())), preferred_element_type=F32)
        for x in range(4):
            for zl in range(2):
                at = (x * 2 + zl) * 8
                half = (yc % 2) * 8
                first[zl * 2 + yc // 4, (yc // 2) % 2, x, half : half + 8, :] = part[at : at + 8, :]


def second_kernel(pos, g, mixed, first, parts, flat, mixw):
    parts[:, :, :, 0] = first[...]
    for k in range(16):
        lanes = slice(k * SLAB, (k + 1) * SLAB)
        flat[:, lanes] = g[:, :, k // 8, k % 8].reshape(ROWS, SLAB)
        mixw[:, lanes] = mixed[:, :, k // 8, k % 8].reshape(ROWS, SLAB)
    for zh in range(4):
        part = lax.dot_general(
            flat[zh * 128 : (zh + 1) * 128, :], mixw[...], (((1,), (1,)), ((), ())), preferred_element_type=F32
        )
        for y in range(4):
            for core in range(2):
                at = (y * 2 + core) * 16
                parts[y, core, zh, 1] = part[at : at + 16, :]


def sum_kernel(pos, parts, out):
    total = parts[0]
    for k in range(1, 32):
        total = total + parts[k]
    place = lax.broadcasted_iota(jnp.int32, (ROWS, ROWS), 0)
    row = lax.broadcasted_iota(jnp.int32, (ROWS, ROWS), 1)
    want = ((row >> 4) & 7) * 64 + ((row >> 2) & 3) * 16 + (row >> 7) * 4 + (row & 3)
    order = (place == want).astype(F32)
    out[0] = total[0] * (ROWS**-0.5 * SLAB**-0.5)
    second = jnp.dot(total[1], order, precision=lax.Precision.HIGHEST, preferred_element_type=F32)
    out[1] = second * (COLS**-0.5 * SLAB**-0.5)


def shifts(count):
    return lambda s: [(k, (k + s) % count) for k in range(count)]


def local(tokens, gate, upstream, first_factor, second_factor):
    zh, zl = lax.axis_index("zh"), lax.axis_index("zl")
    x, yc = lax.axis_index("x"), lax.axis_index("y") * 2 + lax.axis_index("core")
    z = zh * 2 + zl
    pos = jnp.stack([x, z, yc]).astype(jnp.int32)

    sent = gate_call(gate, upstream)
    grad = lax.all_to_all(sent.reshape(64, 8, 16, SLAB), ZYC, 0, 0, tiled=True).reshape(4, 8, 2, 8, 16, SLAB)

    x_step, yc_step, z_step = shifts(4), shifts(8), shifts(8)
    both = jnp.concatenate([first_factor, second_factor], 0)
    eighth = lax.dynamic_slice_in_dim(both, yc * 64, 64, 1)
    got = eighth
    for s in range(1, 4):
        came = lax.ppermute(eighth, ("zh", "x"), [(k * 4 + k, k * 4 + (k + s) % 4) for k in range(4)])
        got = jnp.where(x == (zh + s) % 4, came, got)
    eighths = [got] + [lax.ppermute(got, ("y", "core"), yc_step(s)) for s in range(1, 8)]
    f1, f2t, f1tp = call(
        factor_kernel,
        [shape(COLS, COLS), shape(ROWS, ROWS), shape(COLS, COLS)],
        [pltpu.VMEM((2, COLS, COLS), F32)],
        n_in=8,
    )(pos, *eighths)

    tok_x = []
    for s in range(4):
        piece = lax.dynamic_slice_in_dim(tokens, ((x + s) % 4) * 4, 4, 0)
        tok_x.append(piece if s == 0 else lax.ppermute(piece, "x", x_step(s)))
    tok_cut = call(token_cut_kernel, [shape(4, 4, 64, SLAB)] * 8, n_in=4)(pos, *tok_x)

    tok_cut, grad, f2t, f1tp, f1 = lax.optimization_barrier((tok_cut, grad, f2t, f1tp, f1))
    mg_sent = call(
        second_apply_kernel,
        shape(8, 4, 4, 4, 16, SLAB),
        [pltpu.VMEM((ROWS, 16 * SLAB), BF), pltpu.VMEM((128 * 16, SLAB), F32)],
        n_in=2,
        flops=1 << 30,
    )(pos, f2t, grad)
    tok_z = [tok_cut[0]] + [lax.ppermute(tok_cut[t], ("zh", "zl"), z_step(t)) for t in range(1, 8)]
    mg = lax.all_to_all(mg_sent.reshape(32, 16, 16, SLAB), PLANE, 0, 0, tiled=True).reshape(8, 4, 4, 4, 16, SLAB)

    tg_sent = call(first_apply_kernel, [shape(4, 4, 2, 64, SLAB)] * 4, n_in=2, flops=1 << 30)(pos, f1tp, mg)
    tg_sent, mg = lax.optimization_barrier((tg_sent, mg))
    tg_x = [tg_sent[0]] + [lax.ppermute(tg_sent[s], "x", x_step(s)) for s in range(1, 4)]
    tg_cut = call(grad_cut_kernel, [shape(4, 4, 64, SLAB)] * 8, n_in=4)(pos, *tg_x)
    wide = pltpu.VMEM((ROWS, 16 * SLAB), BF)
    mixed_sent, tokw = call(
        mix_kernel,
        [shape(8, 4, 2, 8, 16, SLAB), shape(COLS, 16 * SLAB)],
        [pltpu.VMEM((4, 4, 4, 2, 64, SLAB), BF), pltpu.VMEM((128 * 16, SLAB), F32)],
        n_in=9,
        flops=1 << 30,
    )(pos, f1, *tok_z)
    tg_cut, mixed_sent = lax.optimization_barrier((tg_cut, mixed_sent))
    tg_z = [tg_cut[0]] + [lax.ppermute(tg_cut[t], ("zh", "zl"), z_step(t)) for t in range(1, 8)]
    mixed = lax.all_to_all(mixed_sent.reshape(32, 16, 16, SLAB), PLANE, 0, 0, tiled=True).reshape(8, 4, 2, 8, 16, SLAB)
    first_part = call(first_kernel, shape(4, 2, 4, 16, COLS, dtype=F32), [wide], n_in=2, flops=1 << 30)(pos, mg, tokw)
    mixed, first_part, tg_z[3:6] = lax.optimization_barrier((mixed, first_part, tg_z[3:6]))
    parts = call(
        second_kernel, shape(4, 2, 4, 2, 16, ROWS, dtype=F32), [wide, wide], n_in=3, flops=1 << 30
    )(pos, grad, mixed, first_part)
    parts = lax.all_to_all(parts.reshape(32, 2, 16, 512), PLANE, 0, 0, tiled=True)
    parts, tg_z = lax.optimization_barrier((parts, tg_z))
    sums = call(sum_kernel, shape(2, 16, 512, dtype=F32))(pos, parts)
    sums = lax.ppermute(sums, ("zh", "x"), [(a * 4 + b, b * 4 + a) for a in range(4) for b in range(4)])
    token_grad = call(grad_join_kernel, shape(16, 64, 1024), n_in=8)(pos, *tg_z)
    return token_grad, sums[:1], sums[1:]


def solution(mesh):
    fine = Mesh(mesh.devices.reshape(4, 4, 2, 4, 2), ("zh", "y", "core", "x", "zl"))
    outer, inner = ("zh", "y", "core"), ("x", "zl")
    grid = P(outer, inner, None)
    factor = P(inner, None, None)
    return jax.shard_map(
        local,
        mesh=fine,
        in_specs=(grid, grid, grid, factor, factor),
        out_specs=(grid, P(inner, outer, None), P(inner, outer, None)),
        check_vma=False,
    )
```

```python
import functools

import jax
import jax.numpy as jnp
from jax import lax
from jax.experimental import pallas as pl
from jax.experimental.pallas import tpu as pltpu
from jax.sharding import Mesh, PartitionSpec as P

ROWS = 512
COLS = 512
SLAB = 128
BF = jnp.bfloat16
F32 = jnp.float32
ZYC = ("zh", "y", "core", "zl")
ZX = ("zh", "x", "zl")
PLANE = ("y", "core", "x")
PARAMS = pltpu.CompilerParams(vmem_limit_bytes=48 * 1024 * 1024)
VM = pl.BlockSpec(memory_space=pltpu.VMEM)
SM = pl.BlockSpec(memory_space=pltpu.SMEM)


def call(kernel, outs, scratch=(), n_in=1, flops=0, moved=4 << 20):
    return pl.pallas_call(
        kernel,
        out_shape=outs,
        in_specs=[SM] + [VM] * n_in,
        out_specs=jax.tree.map(lambda _: VM, outs),
        scratch_shapes=list(scratch),
        compiler_params=PARAMS,
        cost_estimate=pl.CostEstimate(flops=flops, bytes_accessed=moved, transcendentals=0),
    )


def shape(*dims, dtype=BF):
    return jax.ShapeDtypeStruct(dims, dtype)


def gate_kernel(gate, up, out):
    for k in range(8):
        lanes = slice(k * SLAB, (k + 1) * SLAB)
        prod = gate[:, :, lanes].astype(F32) * up[:, :, lanes].astype(F32)
        out[k // 2, :, k % 2] = jnp.swapaxes(prod, 0, 1).astype(BF).reshape(2, 8, 16, SLAB)


def gate_call(gate, up):
    return pl.pallas_call(
        gate_kernel,
        grid=(4,),
        out_shape=shape(4, 8, 2, 8, 16, SLAB),
        in_specs=[pl.BlockSpec((16, 16, 1024), lambda c: (0, c, 0))] * 2,
        out_specs=pl.BlockSpec((4, 2, 2, 8, 16, SLAB), lambda c: (0, c, 0, 0, 0, 0)),
        compiler_params=PARAMS,
        cost_estimate=pl.CostEstimate(flops=1 << 20, bytes_accessed=6 << 20, transcendentals=0),
    )(gate, up)


def factor_kernel(pos, *refs):
    f1, f2t, f1tp, full = refs[4:]
    for k in range(4):
        rows = pl.ds(pl.multiple_of((pos[2] ^ k) * 128, 128), 128)
        full[:, rows, :] = refs[k][...].astype(F32)
    f1[...] = full[0].astype(BF)
    f2t[...] = full[1].T.astype(BF)
    ordered = jnp.concatenate(
        [
            full[0, x * 128 + zl * 64 + c * 8 : x * 128 + zl * 64 + c * 8 + 8, :]
            for x in range(4)
            for c in range(8)
            for zl in range(2)
        ],
        axis=0,
    )
    f1tp[...] = ordered.T.astype(BF)


def second_apply_kernel(pos, f2t, g, *refs):
    outs, flat, swap = refs[:8], refs[8], refs[9]
    for k in range(16):
        flat[:, k * SLAB : (k + 1) * SLAB] = g[:, :, k // 8, k % 8].reshape(ROWS, SLAB)

    def body(zh, _):
        rows = pl.ds(pl.multiple_of(zh * 128, 128), 128)
        for k in range(0, 16, 2):
            part = jnp.dot(f2t[rows, :], flat[:, k * SLAB : (k + 2) * SLAB], preferred_element_type=F32)
            swap[pl.ds(k, 128, stride=16), :] = part[:, :SLAB]
            swap[pl.ds(k + 1, 128, stride=16), :] = part[:, SLAB:]
        for t, out in enumerate(outs):
            at = pl.multiple_of(lax.rem(pos[3] + t, 8) * 256, 256)
            tile = swap[pl.ds(at, 256), :].astype(BF).reshape(4, 4, 16, SLAB)
            for x in range(4):
                out[x, zh] = tile[x]
        return 0

    lax.fori_loop(0, 4, body, 0)


def second_cut_kernel(pos, *refs):
    for s, out in enumerate(refs[8:]):
        owner = lax.rem(pos[0] + s, 4)
        for t in range(8):
            out[lax.rem(pos[3] + 8 - t, 8)] = refs[t][owner]


def first_apply_kernel(pos, f1t, m0, m1, m2, m3, out, mgw):
    for k in range(16):
        for s, block in enumerate((m0, m1, m2, m3)):
            rows = pl.ds(pl.multiple_of(lax.rem(pos[0] + 4 - s, 4) * 128, 128), 128)
            mgw[rows, k * SLAB : (k + 1) * SLAB] = block[:, k // 4, k % 4].reshape(128, SLAB)
    for k in range(0, 16, 2):
        part = jnp.dot(f1t[...], mgw[:, k * SLAB : (k + 2) * SLAB], preferred_element_type=F32).astype(BF)
        out[k // 4, :, :, k % 4] = part[:, :SLAB].reshape(4, 2, 64, SLAB)
        out[k // 4, :, :, k % 4 + 1] = part[:, SLAB:].reshape(4, 2, 64, SLAB)


def token_cut_kernel(tok, out, sem):
    copies = [
        pltpu.make_async_copy(
            tok.at[pl.ds(4 * x, 4), :, pl.ds(SLAB * k, SLAB)], out.at[k // 2, x, k % 2], sem.at[k, x]
        )
        for k in range(8)
        for x in range(4)
    ]
    for copy in copies:
        copy.start()
    for copy in copies:
        copy.wait()


def grad_join_kernel(part, out):
    for k in range(8):
        out[:, :, k * SLAB : (k + 1) * SLAB] = part[k // 2, 0, k % 2]


def grad_join(parts):
    return pl.pallas_call(
        grad_join_kernel,
        grid=(4,),
        out_shape=shape(16, 64, 1024),
        in_specs=[pl.BlockSpec((4, 1, 2, 4, 64, SLAB), lambda x: (0, x, 0, 0, 0, 0))],
        out_specs=pl.BlockSpec((4, 64, 1024), lambda x: (x, 0, 0)),
        compiler_params=PARAMS,
        cost_estimate=pl.CostEstimate(flops=0, bytes_accessed=4 << 20, transcendentals=0),
    )(parts)


def move(kernel, out, operand):
    return pl.pallas_call(
        kernel,
        out_shape=out,
        in_specs=[pl.BlockSpec(memory_space=pl.ANY)],
        out_specs=pl.BlockSpec(memory_space=pl.ANY),
        scratch_shapes=[pltpu.SemaphoreType.DMA((8, 4))],
        compiler_params=PARAMS,
        cost_estimate=pl.CostEstimate(flops=0, bytes_accessed=4 << 20, transcendentals=0),
    )(operand)


def mix_kernel(pos, f1, tok, mixed, tokw, swap):
    for k in range(16):
        tokw[:, k * SLAB : (k + 1) * SLAB] = tok[k // 4, :, :, k % 4].reshape(COLS, SLAB)

    def body(b, _):
        rows = pl.ds(pl.multiple_of(b * 128, 128), 128)
        for k in range(0, 16, 2):
            part = jnp.dot(f1[rows, :], tokw[:, k * SLAB : (k + 2) * SLAB], preferred_element_type=F32)
            swap[pl.ds(k, 128, stride=16), :] = part[:, :SLAB]
            swap[pl.ds(k + 1, 128, stride=16), :] = part[:, SLAB:]
        for zl in range(2):
            tile = swap[zl * 1024 : (zl + 1) * 1024, :].astype(BF).reshape(8, 8, 16, SLAB)
            for yc in range(8):
                mixed[yc, b, zl] = tile[yc]
        return 0

    lax.fori_loop(0, 4, body, 0)


def first_kernel(pos, mgw, tok, keep, give, tokw):
    for k in range(16):
        tokw[:, k * SLAB : (k + 1) * SLAB] = tok[k // 4, :, :, k % 4].reshape(COLS, SLAB)
    for x in range(4):
        left = mgw[x * 128 : (x + 1) * 128, :]
        part = lax.dot_general(left, tokw[...], (((1,), (1,)), ((), ())), preferred_element_type=F32)

        def put(cores):
            for yc in range(8):
                for zl in range(2):
                    at, half = yc * 16 + zl * 8, (yc % 2) * 8
                    cores[(yc // 2) % 2][zl * 2 + yc // 4, x, half : half + 8, :] = part[at : at + 8, :]

        @pl.when(pos[5] == 0)
        def _():
            put((keep, give))

        @pl.when(pos[5] == 1)
        def _():
            put((give, keep))


def second_kernel(pos, g, mixed, keep, give, flat, mixw):
    core = pos[5]
    for k in range(16):
        lanes = slice(k * SLAB, (k + 1) * SLAB)
        flat[:, lanes] = g[:, :, k // 8, k % 8].reshape(ROWS, SLAB)
        mixw[:, lanes] = mixed[:, :, k // 8, k % 8].reshape(ROWS, SLAB)
    for zh in range(4):
        part = lax.dot_general(
            flat[zh * 128 : (zh + 1) * 128, :], mixw[...], (((1,), (1,)), ((), ())), preferred_element_type=F32
        )

        def put(keep, give):
            for y in range(4):
                keep[y, zh] = part[y * 32 : y * 32 + 16, :]
                give[y, zh] = part[y * 32 + 16 : y * 32 + 32, :]

        @pl.when(core == 0)
        def _():
            put(keep, give)

        @pl.when(core == 1)
        def _():
            put(give, keep)


def core_sum_kernel(pos, f, fo, s, so, *outs):
    for t, out in enumerate(outs):
        y = lax.rem(pos[4] + t, 4)
        out[:, 0] = f[y] + fo[y]
        out[:, 1] = s[y] + so[y]


def y_sum_kernel(pos, a, b, c, d, *outs):
    for s, out in enumerate(outs):
        x = lax.rem(pos[0] + s, 4)
        out[...] = (a[x] + b[x]) + (c[x] + d[x])


def sum_kernel(pos, a, b, c, d, out):
    place = lax.broadcasted_iota(jnp.int32, (ROWS, ROWS), 0)
    row = lax.broadcasted_iota(jnp.int32, (ROWS, ROWS), 1)
    want = ((row >> 4) & 7) * 64 + ((row >> 2) & 3) * 16 + (row >> 7) * 4 + (row & 3)
    order = (place == want).astype(F32)
    out[0] = ((a[0] + b[0]) + (c[0] + d[0])) * (ROWS**-0.5 * SLAB**-0.5)
    total = (a[1] + b[1]) + (c[1] + d[1])
    second = jnp.dot(total, order, precision=lax.Precision.HIGHEST, preferred_element_type=F32)
    out[1] = second * (COLS**-0.5 * SLAB**-0.5)


def shifts(count):
    return lambda s: [(k, (k + s) % count) for k in range(count)]


def local(tokens, gate, upstream, first_factor, second_factor):
    zh, zl = lax.axis_index("zh"), lax.axis_index("zl")
    x, y, core = lax.axis_index("x"), lax.axis_index("y"), lax.axis_index("core")
    z, yc, part = zh * 2 + zl, y * 2 + core, (y % 2) * 2 + core
    pos = jnp.stack([x, z, part, yc, y, core]).astype(jnp.int32)
    four, eight = shifts(4), shifts(8)
    wide = pltpu.VMEM((ROWS, 16 * SLAB), BF)
    swap = pltpu.VMEM((128 * 16, SLAB), F32)
    f32 = functools.partial(shape, dtype=F32)

    gated = gate_call(gate, upstream)
    grad = lax.all_to_all(gated.reshape(64, 8, 16, SLAB), ZYC, 0, 0, tiled=True).reshape(4, 8, 2, 8, 16, SLAB)
    sent = move(token_cut_kernel, shape(4, 4, 2, 4, 64, SLAB), tokens)

    both = jnp.concatenate([first_factor, second_factor], 0)
    quarter = lax.dynamic_slice_in_dim(both, part * 128, 128, 1)
    got = quarter
    for s in range(1, 4):
        came = lax.ppermute(quarter, ("zh", "x"), [(k * 4 + k, k * 4 + (k + s) % 4) for k in range(4)])
        got = jnp.where(x == (zh + s) % 4, came, got)
    quarters = [got] + [lax.ppermute(got, ("y", "core"), [(k, k ^ s) for k in range(8)]) for s in range(1, 4)]
    f1, f2t, f1tp = call(
        factor_kernel,
        [shape(COLS, COLS), shape(ROWS, ROWS), shape(COLS, COLS)],
        [pltpu.VMEM((2, COLS, COLS), F32)],
        n_in=4,
    )(pos, *quarters)
    sent, grad, f1, f2t, f1tp = lax.optimization_barrier((sent, grad, f1, f2t, f1tp))

    tok = lax.all_to_all(sent.reshape(32, 4, 64, SLAB), ZX, 0, 0, tiled=True).reshape(4, 4, 2, 4, 64, SLAB)
    mg = call(second_apply_kernel, [shape(4, 4, 4, 16, SLAB)] * 8, [wide, swap], n_in=2, flops=1 << 30)(pos, f2t, grad)
    mg = [mg[0]] + [lax.ppermute(mg[t], ("y", "core"), eight(t)) for t in range(1, 8)]
    mg = call(second_cut_kernel, [shape(8, 4, 4, 16, SLAB)] * 4, n_in=8)(pos, *mg)
    mg = [mg[0]] + [lax.ppermute(mg[s], "x", four(s)) for s in range(1, 4)]
    tok, mg = lax.optimization_barrier((tok, mg))

    mixed = call(mix_kernel, shape(8, 4, 2, 8, 16, SLAB), [wide, swap], n_in=2, flops=1 << 30)(pos, f1, tok)
    mixed = lax.all_to_all(mixed.reshape(32, 16, 16, SLAB), PLANE, 0, 0, tiled=True).reshape(8, 4, 2, 8, 16, SLAB)
    sent, mgw = call(
        first_apply_kernel, [shape(4, 4, 2, 4, 64, SLAB), shape(COLS, 16 * SLAB)], n_in=5, flops=1 << 30
    )(pos, f1tp, *mg)
    mixed, sent = lax.optimization_barrier((mixed, sent))

    home = lax.all_to_all(sent.reshape(32, 4, 64, SLAB), ZX, 0, 0, tiled=True)
    halves = [f32(4, 4, 16, 512)] * 2
    second_keep, second_give = call(second_kernel, halves, [wide, wide], n_in=2, flops=1 << 30)(pos, grad, mixed)
    first_keep, first_give = call(first_kernel, halves, [wide], n_in=2, flops=1 << 30)(pos, mgw, tok)
    other = [(0, 1), (1, 0)]
    first_came, second_came = lax.ppermute(first_give, "core", other), lax.ppermute(second_give, "core", other)
    sums = call(core_sum_kernel, [f32(4, 2, 16, 512)] * 4, n_in=4)(
        pos, first_keep, first_came, second_keep, second_came
    )
    sums = [sums[0]] + [lax.ppermute(sums[t], "y", four(t)) for t in range(1, 4)]
    sums = call(y_sum_kernel, [f32(2, 16, 512)] * 4, n_in=4, moved=1 << 20)(pos, *sums)
    sums = [sums[0]] + [lax.ppermute(sums[s], "x", four(s)) for s in range(1, 4)]
    sums = call(sum_kernel, f32(2, 16, 512), n_in=4, moved=1 << 19)(pos, *sums)
    sums = lax.ppermute(sums, ("zh", "x"), [(a * 4 + b, b * 4 + a) for a in range(4) for b in range(4)])
    home, sums = lax.optimization_barrier((home, sums))
    token_grad = grad_join(home.reshape(4, 4, 2, 4, 64, SLAB))
    return token_grad, sums[:1], sums[1:]


def solution(mesh):
    fine = Mesh(mesh.devices.reshape(4, 4, 2, 4, 2), ("zh", "y", "core", "x", "zl"))
    outer, inner = ("zh", "y", "core"), ("x", "zl")
    grid = P(outer, inner, None)
    factor = P(inner, None, None)
    return jax.shard_map(
        local,
        mesh=fine,
        in_specs=(grid, grid, grid, factor, factor),
        out_specs=(grid, P(inner, outer, None), P(inner, outer, None)),
        check_vma=False,
    )
```

```python
import functools

import jax
import jax.numpy as jnp
from jax import lax
from jax.experimental import pallas as pl
from jax.experimental.pallas import tpu as pltpu
from jax.sharding import Mesh, PartitionSpec as P

ROWS = 512
COLS = 512
SLAB = 128
BF = jnp.bfloat16
F32 = jnp.float32
ZYC = ("zh", "y", "core", "zl")
ZX = ("zh", "x", "zl")
PLANE = ("y", "core", "x")
NEAR, FAR = (0, 1, 7, 2), (6, 3, 5, 4)
PARAMS = pltpu.CompilerParams(vmem_limit_bytes=48 * 1024 * 1024)
VM = pl.BlockSpec(memory_space=pltpu.VMEM)
SM = pl.BlockSpec(memory_space=pltpu.SMEM)
HB = pl.BlockSpec(memory_space=pltpu.HBM)


def call(kernel, outs, scratch=(), n_in=1, hbm=(), flops=0, moved=4 << 20):
    return pl.pallas_call(
        kernel,
        out_shape=outs,
        in_specs=[SM] + [HB if k in hbm else VM for k in range(n_in)],
        out_specs=jax.tree.map(lambda _: HB if "out" in hbm else VM, outs),
        scratch_shapes=list(scratch),
        compiler_params=PARAMS,
        cost_estimate=pl.CostEstimate(flops=flops, bytes_accessed=moved, transcendentals=0),
    )


def shape(*dims, dtype=BF):
    return jax.ShapeDtypeStruct(dims, dtype)


def gate_kernel(gate, up, out):
    for k in range(8):
        lanes = slice(k * SLAB, (k + 1) * SLAB)
        prod = gate[:, :, lanes].astype(F32) * up[:, :, lanes].astype(F32)
        out[k // 2, :, k % 2] = jnp.swapaxes(prod, 0, 1).astype(BF).reshape(2, 8, 16, SLAB)


def gate_call(gate, up):
    return pl.pallas_call(
        gate_kernel,
        grid=(4,),
        out_shape=shape(4, 8, 2, 8, 16, SLAB),
        in_specs=[pl.BlockSpec((16, 16, 1024), lambda c: (0, c, 0))] * 2,
        out_specs=pl.BlockSpec((4, 2, 2, 8, 16, SLAB), lambda c: (0, c, 0, 0, 0, 0)),
        compiler_params=PARAMS,
        cost_estimate=pl.CostEstimate(flops=1 << 20, bytes_accessed=6 << 20, transcendentals=0),
    )(gate, up)


def second_factor_kernel(pos, *refs):
    f2t, full = refs[4:]
    for k in range(4):
        rows = pl.ds(pl.multiple_of((pos[2] ^ k) * 128, 128), 128)
        full[rows, :] = refs[k][0].astype(F32)
    f2t[...] = full[...].T.astype(BF)


def first_factor_kernel(pos, *refs):
    f1, f1tp, full = refs[4:]
    for k in range(4):
        rows = pl.ds(pl.multiple_of((pos[2] ^ k) * 128, 128), 128)
        full[rows, :] = refs[k][0].astype(F32)
    f1[...] = full[...].astype(BF)
    ordered = jnp.concatenate(
        [
            full[x * 128 + zl * 64 + c * 8 : x * 128 + zl * 64 + c * 8 + 8, :]
            for x in range(4)
            for c in range(8)
            for zl in range(2)
        ],
        axis=0,
    )
    f1tp[...] = ordered.T.astype(BF)


def bring(g, flat, sem):
    copies = [
        pltpu.make_async_copy(
            g.at[:, :, k // 8, k % 8], flat.at[:, :, :, pl.ds(k * SLAB, SLAB)], sem.at[k]
        )
        for k in range(16)
    ]
    for copy in copies:
        copy.start()
    return copies


def second_apply_kernel(pos, f2t, g, *refs):
    outs, flat, swap, sem = refs[:8], refs[8], refs[9], refs[10]
    for copy in bring(g, flat, sem):
        copy.wait()

    def body(zh, _):
        rows = pl.ds(pl.multiple_of(zh * 128, 128), 128)
        for k in range(0, 16, 2):
            right = flat[:, :, :, k * SLAB : (k + 2) * SLAB].reshape(ROWS, 2 * SLAB)
            part = jnp.dot(f2t[rows, :], right, preferred_element_type=F32)
            swap[pl.ds(k, 128, stride=16), :] = part[:, :SLAB]
            swap[pl.ds(k + 1, 128, stride=16), :] = part[:, SLAB:]
        for t, out in enumerate(outs):
            at = pl.multiple_of(lax.rem(pos[3] + t, 8) * 256, 256)
            tile = swap[pl.ds(at, 256), :].astype(BF).reshape(4, 4, 16, SLAB)
            for x in range(4):
                out[x, zh] = tile[x]
        return 0

    lax.fori_loop(0, 4, body, 0)


def second_cut_kernel(pos, a, b, c, d, *outs):
    for s, out in enumerate(outs):
        owner = lax.rem(pos[0] + s, 4)
        for t, block in enumerate((a, b, c, d)):
            out[t] = block[owner]


def first_apply_kernel(pos, f1t, *refs):
    out, mgw = refs[8:]
    for i, steps in enumerate((NEAR, FAR)):
        for s in range(4):
            block = refs[i * 4 + s]
            for j, t in enumerate(steps):
                at = lax.rem(pos[0] + 4 - s, 4) * 128 + lax.rem(pos[3] + 8 - t, 8) * 16
                rows = pl.ds(pl.multiple_of(at, 16), 16)
                for k in range(16):
                    mgw[rows, k * SLAB : (k + 1) * SLAB] = block[j, k // 4, k % 4]
    for k in range(0, 16, 2):
        part = jnp.dot(f1t[...], mgw[:, k * SLAB : (k + 2) * SLAB], preferred_element_type=F32).astype(BF)
        out[k // 4, :, :, k % 4] = part[:, :SLAB].reshape(4, 2, 64, SLAB)
        out[k // 4, :, :, k % 4 + 1] = part[:, SLAB:].reshape(4, 2, 64, SLAB)


def token_cut_kernel(pos, x0, x1, x2, x3, out):
    for s, block in enumerate((x0, x1, x2, x3)):
        source = lax.rem(pos[0] + 4 - s, 4)
        for k in range(8):
            out[k // 2, k % 2, source] = block[:, :, k * SLAB : (k + 1) * SLAB]


def grad_join_kernel(pos, part, out, stage, arrive, leave):
    def into(x, k):
        return pltpu.make_async_copy(
            part.at[k // 2, x, k % 2], stage.at[pl.ds(4 * x, 4), :, pl.ds(SLAB * k, SLAB)], arrive.at[x, k]
        )

    def away(x):
        rows = pl.ds(4 * x, 4)
        return pltpu.make_async_copy(stage.at[rows], out.at[rows], leave.at[x])

    for x in range(4):
        for k in range(8):
            into(x, k).start()
    for x in range(4):
        for k in range(8):
            into(x, k).wait()
        away(x).start()
    for x in range(4):
        away(x).wait()


def mix_kernel(pos, f1, tok, mixed, tokw, swap, stage, sem):
    for k in range(16):
        for x in range(4):
            for zl in range(2):
                at = (x * 2 + zl) * 64
                tokw[at : at + 64, k * SLAB : (k + 1) * SLAB] = tok[k // 4, zl, x, k % 4]

    def copy(b):
        return pltpu.make_async_copy(stage.at[b], mixed.at[:, b], sem.at[b])

    for b in range(4):
        for k in range(0, 16, 2):
            part = jnp.dot(
                f1[b * 128 : (b + 1) * 128, :], tokw[:, k * SLAB : (k + 2) * SLAB], preferred_element_type=F32
            )
            swap[pl.ds(k, 128, stride=16), :] = part[:, :SLAB]
            swap[pl.ds(k + 1, 128, stride=16), :] = part[:, SLAB:]
        for zl in range(2):
            stage[b, :, zl] = swap[zl * 1024 : (zl + 1) * 1024, :].astype(BF).reshape(8, 8, 16, SLAB)
        copy(b).start()
    for b in range(4):
        copy(b).wait()


def first_kernel(pos, mgw, tok, keep, give, tokw):
    for k in range(16):
        for x in range(4):
            for zl in range(2):
                at = (x * 2 + zl) * 64
                tokw[at : at + 64, k * SLAB : (k + 1) * SLAB] = tok[k // 4, zl, x, k % 4]
    for x in range(4):
        left = mgw[x * 128 : (x + 1) * 128, :]
        part = lax.dot_general(left, tokw[...], (((1,), (1,)), ((), ())), preferred_element_type=F32)

        def put(cores):
            for yc in range(8):
                for zl in range(2):
                    at, half = yc * 16 + zl * 8, (yc % 2) * 8
                    cores[(yc // 2) % 2][zl * 2 + yc // 4, x, half : half + 8, :] = part[at : at + 8, :]

        @pl.when(pos[5] == 0)
        def _():
            put((keep, give))

        @pl.when(pos[5] == 1)
        def _():
            put((give, keep))


def second_kernel(pos, g, mixed, keep, give, flat, mixw, sem):
    core = pos[5]
    copies = bring(g, flat, sem)
    for k in range(16):
        lanes = slice(k * SLAB, (k + 1) * SLAB)
        mixw[:, lanes] = mixed[:, :, k // 8, k % 8].reshape(ROWS, SLAB)
    for copy in copies:
        copy.wait()
    for zh in range(4):
        part = lax.dot_general(
            flat[zh].reshape(128, 16 * SLAB), mixw[...], (((1,), (1,)), ((), ())), preferred_element_type=F32
        )

        def put(keep, give):
            for y in range(4):
                keep[y, zh] = part[y * 32 : y * 32 + 16, :]
                give[y, zh] = part[y * 32 + 16 : y * 32 + 32, :]

        @pl.when(core == 0)
        def _():
            put(keep, give)

        @pl.when(core == 1)
        def _():
            put(give, keep)


def core_sum_kernel(pos, f, fo, s, so, *outs):
    for t, out in enumerate(outs):
        y = lax.rem(pos[4] + t, 4)
        out[:, 0] = f[y] + fo[y]
        out[:, 1] = s[y] + so[y]


def y_sum_kernel(pos, a, b, c, d, *outs):
    for s, out in enumerate(outs):
        x = lax.rem(pos[0] + s, 4)
        out[...] = (a[x] + b[x]) + (c[x] + d[x])


def sum_kernel(pos, a, b, c, d, out):
    place = lax.broadcasted_iota(jnp.int32, (ROWS, ROWS), 0)
    row = lax.broadcasted_iota(jnp.int32, (ROWS, ROWS), 1)
    want = ((row >> 4) & 7) * 64 + ((row >> 2) & 3) * 16 + (row >> 7) * 4 + (row & 3)
    order = (place == want).astype(F32)
    out[0] = ((a[0] + b[0]) + (c[0] + d[0])) * (ROWS**-0.5 * SLAB**-0.5)
    total = (a[1] + b[1]) + (c[1] + d[1])
    second = jnp.dot(total, order, precision=lax.Precision.HIGHEST, preferred_element_type=F32)
    out[1] = second * (COLS**-0.5 * SLAB**-0.5)


def shifts(count):
    return lambda s: [(k, (k + s) % count) for k in range(count)]


def local(tokens, gate, upstream, first_factor, second_factor):
    zh, zl = lax.axis_index("zh"), lax.axis_index("zl")
    x, y, core = lax.axis_index("x"), lax.axis_index("y"), lax.axis_index("core")
    z, yc, part = zh * 2 + zl, y * 2 + core, (y % 2) * 2 + core
    pos = jnp.stack([x, z, part, yc, y, core]).astype(jnp.int32)
    four, eight = shifts(4), shifts(8)
    wide = pltpu.VMEM((ROWS, 16 * SLAB), BF)
    swap = pltpu.VMEM((128 * 16, SLAB), F32)
    cols, dma = pltpu.VMEM((4, 8, 16, 16 * SLAB), BF), pltpu.SemaphoreType.DMA((16,))
    f32 = functools.partial(shape, dtype=F32)

    gated = gate_call(gate, upstream)
    grad = lax.all_to_all(gated.reshape(64, 8, 16, SLAB), ZYC, 0, 0, tiled=True).reshape(4, 8, 2, 8, 16, SLAB)
    tok_x = []
    for s in range(4):
        piece = lax.dynamic_slice_in_dim(tokens, ((x + s) % 4) * 4, 4, 0)
        tok_x.append(piece if s == 0 else lax.ppermute(piece, "x", four(s)))
    sent = call(token_cut_kernel, shape(4, 2, 4, 4, 64, SLAB), n_in=4)(pos, *tok_x)

    both = jnp.concatenate([first_factor, second_factor], 0)
    quarter = lax.dynamic_slice_in_dim(both, part * 128, 128, 1)
    got = quarter
    for s in range(1, 4):
        came = lax.ppermute(quarter, ("zh", "x"), [(k * 4 + k, k * 4 + (k + s) % 4) for k in range(4)])
        got = jnp.where(x == (zh + s) % 4, came, got)

    def gathered(own):
        return [own] + [lax.ppermute(own, ("y", "core"), [(k, k ^ s) for k in range(8)]) for s in range(1, 4)]

    full = pltpu.VMEM((COLS, COLS), F32)
    f2t = call(second_factor_kernel, shape(ROWS, ROWS), [full], n_in=4, moved=1 << 20)(pos, *gathered(got[1:]))
    got, sent, grad, f2t = lax.optimization_barrier((got, sent, grad, f2t))

    tok = lax.all_to_all(sent.reshape(8, 16, 64, SLAB), ("zh", "zl"), 0, 0, tiled=True).reshape(4, 2, 4, 4, 64, SLAB)
    f1, f1tp = call(first_factor_kernel, [shape(COLS, COLS)] * 2, [full], n_in=4, moved=1 << 20)(
        pos, *gathered(got[:1])
    )
    mg = call(second_apply_kernel, [shape(4, 4, 4, 16, SLAB)] * 8, [cols, swap, dma], n_in=2, hbm=(1,), flops=1 << 30)(
        pos, f2t, grad
    )
    crossed = []
    for steps in (NEAR, FAR):
        group = [mg[t] if t == 0 else lax.ppermute(mg[t], ("y", "core"), eight(t)) for t in steps]
        group = call(second_cut_kernel, [shape(4, 4, 4, 16, SLAB)] * 4, n_in=4, moved=1 << 21)(pos, *group)
        crossed += [group[0]] + [lax.ppermute(group[s], "x", four(s)) for s in (2, 1, 3)]
    mg = [crossed[i] for i in (0, 2, 1, 3, 4, 6, 5, 7)]
    tok, mg = lax.optimization_barrier((tok, mg))

    stage = pltpu.VMEM((4, 8, 2, 8, 16, SLAB), BF)
    mixed = call(
        mix_kernel, shape(8, 4, 2, 8, 16, SLAB), [wide, swap, stage, dma], n_in=2, hbm=("out",), flops=1 << 30
    )(pos, f1, tok)
    mixed = lax.all_to_all(mixed.reshape(32, 16, 16, SLAB), PLANE, 0, 0, tiled=True).reshape(8, 4, 2, 8, 16, SLAB)
    sent, mgw = call(
        first_apply_kernel, [shape(4, 4, 2, 4, 64, SLAB), shape(COLS, 16 * SLAB)], n_in=9, flops=1 << 30
    )(pos, f1tp, *mg)
    mixed, sent = lax.optimization_barrier((mixed, sent))

    home = lax.all_to_all(sent.reshape(32, 4, 64, SLAB), ZX, 0, 0, tiled=True)
    halves = [f32(4, 4, 16, 512)] * 2
    second_keep, second_give = call(second_kernel, halves, [cols, wide, dma], n_in=2, hbm=(0,), flops=1 << 30)(
        pos, grad, mixed
    )
    first_keep, first_give = call(first_kernel, halves, [wide], n_in=2, flops=1 << 30)(pos, mgw, tok)
    other = [(0, 1), (1, 0)]
    first_came, second_came = lax.ppermute(first_give, "core", other), lax.ppermute(second_give, "core", other)
    sums = call(core_sum_kernel, [f32(4, 2, 16, 512)] * 4, n_in=4)(
        pos, first_keep, first_came, second_keep, second_came
    )
    sums = [sums[0]] + [lax.ppermute(sums[t], "y", four(t)) for t in range(1, 4)]
    sums = call(y_sum_kernel, [f32(2, 16, 512)] * 4, n_in=4, moved=1 << 20)(pos, *sums)
    sums = [sums[0]] + [lax.ppermute(sums[s], "x", four(s)) for s in range(1, 4)]
    sums = call(sum_kernel, f32(2, 16, 512), n_in=4, moved=1 << 19)(pos, *sums)
    sums = lax.ppermute(sums, ("zh", "x"), [(a * 4 + b, b * 4 + a) for a in range(4) for b in range(4)])
    home, sums = lax.optimization_barrier((home, sums))
    token_grad = call(
        grad_join_kernel,
        shape(16, 64, 1024),
        [pltpu.VMEM((16, 64, 1024), BF), pltpu.SemaphoreType.DMA((4, 8)), pltpu.SemaphoreType.DMA((4,))],
        hbm=(0, "out"),
    )(pos, home.reshape(4, 4, 2, 4, 64, SLAB))
    return token_grad, sums[:1], sums[1:]


def solution(mesh):
    fine = Mesh(mesh.devices.reshape(4, 4, 2, 4, 2), ("zh", "y", "core", "x", "zl"))
    outer, inner = ("zh", "y", "core"), ("x", "zl")
    grid = P(outer, inner, None)
    factor = P(inner, None, None)
    return jax.shard_map(
        local,
        mesh=fine,
        in_specs=(grid, grid, grid, factor, factor),
        out_specs=(grid, P(inner, outer, None), P(inner, outer, None)),
        check_vma=False,
    )
```

```python
import functools

import jax
import jax.numpy as jnp
from jax import lax
from jax.experimental import pallas as pl
from jax.experimental.pallas import tpu as pltpu
from jax.sharding import Mesh, PartitionSpec as P

ROWS = 512
COLS = 512
SLAB = 128
BF = jnp.bfloat16
F32 = jnp.float32
ZYC = ("zh", "y", "core", "zl")
ZX = ("zh", "x", "zl")
PLANE = ("y", "core", "x")
NEAR, FAR = (0, 1, 7, 2), (6, 3, 5, 4)
PARAMS = pltpu.CompilerParams(vmem_limit_bytes=48 * 1024 * 1024)
VM = pl.BlockSpec(memory_space=pltpu.VMEM)
SM = pl.BlockSpec(memory_space=pltpu.SMEM)
HB = pl.BlockSpec(memory_space=pltpu.HBM)


def call(kernel, outs, scratch=(), n_in=1, hbm=(), flops=0, moved=4 << 20):
    return pl.pallas_call(
        kernel,
        out_shape=outs,
        in_specs=[SM] + [HB if k in hbm else VM for k in range(n_in)],
        out_specs=jax.tree.map(lambda _: HB if "out" in hbm else VM, outs),
        scratch_shapes=list(scratch),
        compiler_params=PARAMS,
        cost_estimate=pl.CostEstimate(flops=flops, bytes_accessed=moved, transcendentals=0),
    )


def shape(*dims, dtype=BF):
    return jax.ShapeDtypeStruct(dims, dtype)


def gate_kernel(gate, up, out, swap):
    for k in range(8):
        lanes = slice(k * SLAB, (k + 1) * SLAB)
        for r in range(16):
            swap[k, pl.ds(r, 16, stride=16), :] = gate[r, :, lanes].astype(F32) * up[r, :, lanes].astype(F32)
        out[k // 2, :, k % 2] = swap[k].astype(BF).reshape(2, 8, 16, SLAB)


def gate_call(gate, up):
    return pl.pallas_call(
        gate_kernel,
        grid=(4,),
        out_shape=shape(4, 8, 2, 8, 16, SLAB),
        in_specs=[pl.BlockSpec((16, 16, 1024), lambda c: (0, c, 0))] * 2,
        out_specs=pl.BlockSpec((4, 2, 2, 8, 16, SLAB), lambda c: (0, c, 0, 0, 0, 0)),
        scratch_shapes=[pltpu.VMEM((8, 256, SLAB), F32)],
        compiler_params=PARAMS,
        cost_estimate=pl.CostEstimate(flops=1 << 20, bytes_accessed=6 << 20, transcendentals=0),
    )(gate, up)


def second_factor_kernel(pos, *refs):
    f2t, full = refs[4:]
    for k in range(4):
        rows = pl.ds(pl.multiple_of((pos[2] ^ k) * 128, 128), 128)
        full[rows, :] = refs[k][0].astype(F32)
    f2t[...] = full[...].T.astype(BF)


def first_factor_kernel(pos, *refs):
    f1, f1tp, full = refs[4:]
    for k in range(4):
        rows = pl.ds(pl.multiple_of((pos[2] ^ k) * 128, 128), 128)
        full[rows, :] = refs[k][0].astype(F32)
    f1[...] = full[...].astype(BF)
    ordered = jnp.concatenate(
        [
            full[x * 128 + zl * 64 + c * 8 : x * 128 + zl * 64 + c * 8 + 8, :]
            for x in range(4)
            for c in range(8)
            for zl in range(2)
        ],
        axis=0,
    )
    f1tp[...] = ordered.T.astype(BF)


def second_apply_kernel(pos, f2t, g, *refs):
    outs, flat, swap = refs[:8], refs[8], refs[9]
    for k in range(16):
        flat[:, k * SLAB : (k + 1) * SLAB] = g[:, :, k // 8, k % 8].reshape(ROWS, SLAB)

    def body(zh, _):
        rows = pl.ds(pl.multiple_of(zh * 128, 128), 128)
        for k in range(0, 16, 2):
            part = jnp.dot(f2t[rows, :], flat[:, k * SLAB : (k + 2) * SLAB], preferred_element_type=F32)
            swap[pl.ds(k, 128, stride=16), :] = part[:, :SLAB]
            swap[pl.ds(k + 1, 128, stride=16), :] = part[:, SLAB:]
        for t, out in enumerate(outs):
            at = pl.multiple_of(lax.rem(pos[3] + t, 8) * 256, 256)
            tile = swap[pl.ds(at, 256), :].astype(BF).reshape(4, 4, 16, SLAB)
            for x in range(4):
                out[x, zh] = tile[x]
        return 0

    lax.fori_loop(0, 4, body, 0)


def second_cut_kernel(pos, a, b, c, d, *outs):
    for s, out in enumerate(outs):
        owner = lax.rem(pos[0] + s, 4)
        for t, block in enumerate((a, b, c, d)):
            out[t] = block[owner]


def first_apply_kernel(pos, f1t, *refs):
    out, mgw = refs[8:]
    for i, steps in enumerate((NEAR, FAR)):
        for s in range(4):
            block = refs[i * 4 + s]
            for j, t in enumerate(steps):
                at = lax.rem(pos[0] + 4 - s, 4) * 128 + lax.rem(pos[3] + 8 - t, 8) * 16
                rows = pl.ds(pl.multiple_of(at, 16), 16)
                for k in range(16):
                    mgw[rows, k * SLAB : (k + 1) * SLAB] = block[j, k // 4, k % 4]
    for k in range(0, 16, 2):
        part = jnp.dot(f1t[...], mgw[:, k * SLAB : (k + 2) * SLAB], preferred_element_type=F32).astype(BF)
        out[k // 4, :, :, k % 4] = part[:, :SLAB].reshape(4, 2, 64, SLAB)
        out[k // 4, :, :, k % 4 + 1] = part[:, SLAB:].reshape(4, 2, 64, SLAB)


def token_cut_kernel(pos, x0, x1, x2, x3, out):
    for s, block in enumerate((x0, x1, x2, x3)):
        source = lax.rem(pos[0] + 4 - s, 4)
        for k in range(8):
            out[k // 2, k % 2, source] = block[:, :, k * SLAB : (k + 1) * SLAB]


def grad_join_kernel(pos, part, out, stage, arrive, leave):
    def into(x, k):
        return pltpu.make_async_copy(
            part.at[k // 2, x, k % 2], stage.at[pl.ds(4 * x, 4), :, pl.ds(SLAB * k, SLAB)], arrive.at[x, k]
        )

    def away(x):
        rows = pl.ds(4 * x, 4)
        return pltpu.make_async_copy(stage.at[rows], out.at[rows], leave.at[x])

    for x in range(4):
        for k in range(8):
            into(x, k).start()
    for x in range(4):
        for k in range(8):
            into(x, k).wait()
        away(x).start()
    for x in range(4):
        away(x).wait()


def mix_kernel(pos, f1, tok, mixed, tokw, swap, stage, sem):
    for k in range(16):
        for x in range(4):
            for zl in range(2):
                at = (x * 2 + zl) * 64
                tokw[at : at + 64, k * SLAB : (k + 1) * SLAB] = tok[k // 4, zl, x, k % 4]

    def copy(b):
        return pltpu.make_async_copy(stage.at[b], mixed.at[:, b], sem.at[b])

    for b in range(4):
        for k in range(0, 16, 2):
            part = jnp.dot(
                f1[b * 128 : (b + 1) * 128, :], tokw[:, k * SLAB : (k + 2) * SLAB], preferred_element_type=F32
            )
            swap[pl.ds(k, 128, stride=16), :] = part[:, :SLAB]
            swap[pl.ds(k + 1, 128, stride=16), :] = part[:, SLAB:]
        for zl in range(2):
            stage[b, :, zl] = swap[zl * 1024 : (zl + 1) * 1024, :].astype(BF).reshape(8, 8, 16, SLAB)
        copy(b).start()
    for b in range(4):
        copy(b).wait()


def first_kernel(pos, mgw, tok, keep, give, tokw):
    for k in range(16):
        for x in range(4):
            for zl in range(2):
                at = (x * 2 + zl) * 64
                tokw[at : at + 64, k * SLAB : (k + 1) * SLAB] = tok[k // 4, zl, x, k % 4]
    for x in range(4):
        left = mgw[x * 128 : (x + 1) * 128, :]
        part = lax.dot_general(left, tokw[...], (((1,), (1,)), ((), ())), preferred_element_type=F32)

        def put(cores):
            for yc in range(8):
                for zl in range(2):
                    at, half = yc * 16 + zl * 8, (yc % 2) * 8
                    cores[(yc // 2) % 2][zl * 2 + yc // 4, x, half : half + 8, :] = part[at : at + 8, :]

        @pl.when(pos[5] == 0)
        def _():
            put((keep, give))

        @pl.when(pos[5] == 1)
        def _():
            put((give, keep))


def second_kernel(pos, flat, mixed, keep, give, mixw):
    core = pos[5]
    for k in range(16):
        lanes = slice(k * SLAB, (k + 1) * SLAB)
        mixw[:, lanes] = mixed[:, :, k // 8, k % 8].reshape(ROWS, SLAB)
    for zh in range(4):
        part = lax.dot_general(
            flat[zh * 128 : (zh + 1) * 128, :], mixw[...], (((1,), (1,)), ((), ())), preferred_element_type=F32
        )

        def put(keep, give):
            for y in range(4):
                keep[y, zh] = part[y * 32 : y * 32 + 16, :]
                give[y, zh] = part[y * 32 + 16 : y * 32 + 32, :]

        @pl.when(core == 0)
        def _():
            put(keep, give)

        @pl.when(core == 1)
        def _():
            put(give, keep)


def core_sum_kernel(pos, f, fo, s, so, *outs):
    for t, out in enumerate(outs):
        y = lax.rem(pos[4] + t, 4)
        out[:, 0] = f[y] + fo[y]
        out[:, 1] = s[y] + so[y]


def y_sum_kernel(pos, a, b, c, d, *outs):
    for s, out in enumerate(outs):
        x = lax.rem(pos[0] + s, 4)
        out[...] = (a[x] + b[x]) + (c[x] + d[x])


def sum_kernel(pos, a, b, c, d, out):
    place = lax.broadcasted_iota(jnp.int32, (ROWS, ROWS), 0)
    row = lax.broadcasted_iota(jnp.int32, (ROWS, ROWS), 1)
    want = ((row >> 4) & 7) * 64 + ((row >> 2) & 3) * 16 + (row >> 7) * 4 + (row & 3)
    order = (place == want).astype(F32)
    out[0] = ((a[0] + b[0]) + (c[0] + d[0])) * (ROWS**-0.5 * SLAB**-0.5)
    total = (a[1] + b[1]) + (c[1] + d[1])
    second = jnp.dot(total, order, precision=lax.Precision.HIGHEST, preferred_element_type=F32)
    out[1] = second * (COLS**-0.5 * SLAB**-0.5)


def shifts(count):
    return lambda s: [(k, (k + s) % count) for k in range(count)]


def local(tokens, gate, upstream, first_factor, second_factor):
    zh, zl = lax.axis_index("zh"), lax.axis_index("zl")
    x, y, core = lax.axis_index("x"), lax.axis_index("y"), lax.axis_index("core")
    z, yc, part = zh * 2 + zl, y * 2 + core, (y % 2) * 2 + core
    pos = jnp.stack([x, z, part, yc, y, core]).astype(jnp.int32)
    four, eight = shifts(4), shifts(8)
    wide = pltpu.VMEM((ROWS, 16 * SLAB), BF)
    swap = pltpu.VMEM((128 * 16, SLAB), F32)
    f32 = functools.partial(shape, dtype=F32)

    gated = gate_call(gate, upstream)
    grad = lax.all_to_all(gated.reshape(64, 8, 16, SLAB), ZYC, 0, 0, tiled=True).reshape(4, 8, 2, 8, 16, SLAB)
    tok_x = []
    for s in range(4):
        piece = lax.dynamic_slice_in_dim(tokens, ((x + s) % 4) * 4, 4, 0)
        tok_x.append(piece if s == 0 else lax.ppermute(piece, "x", four(s)))
    sent = call(token_cut_kernel, shape(4, 2, 4, 4, 64, SLAB), n_in=4)(pos, *tok_x)

    both = jnp.concatenate([first_factor, second_factor], 0)
    quarter = lax.dynamic_slice_in_dim(both, part * 128, 128, 1)
    got = quarter
    for s in range(1, 4):
        came = lax.ppermute(quarter, ("zh", "x"), [(k * 4 + k, k * 4 + (k + s) % 4) for k in range(4)])
        got = jnp.where(x == (zh + s) % 4, came, got)

    def gathered(own):
        return [own] + [lax.ppermute(own, ("y", "core"), [(k, k ^ s) for k in range(8)]) for s in range(1, 4)]

    full = pltpu.VMEM((COLS, COLS), F32)
    f2t = call(second_factor_kernel, shape(ROWS, ROWS), [full], n_in=4, moved=1 << 20)(pos, *gathered(got[1:]))
    got, sent, grad, f2t = lax.optimization_barrier((got, sent, grad, f2t))

    tok = lax.all_to_all(sent.reshape(8, 16, 64, SLAB), ("zh", "zl"), 0, 0, tiled=True).reshape(4, 2, 4, 4, 64, SLAB)
    f1, f1tp = call(first_factor_kernel, [shape(COLS, COLS)] * 2, [full], n_in=4, moved=1 << 20)(
        pos, *gathered(got[:1])
    )
    *mg, flat = call(
        second_apply_kernel,
        [shape(4, 4, 4, 16, SLAB)] * 8 + [shape(ROWS, 16 * SLAB)],
        [swap],
        n_in=2,
        flops=1 << 30,
    )(pos, f2t, grad)
    crossed = []
    for steps in (NEAR, FAR):
        group = [mg[t] if t == 0 else lax.ppermute(mg[t], ("y", "core"), eight(t)) for t in steps]
        group = call(second_cut_kernel, [shape(4, 4, 4, 16, SLAB)] * 4, n_in=4, moved=1 << 21)(pos, *group)
        crossed += [group[0]] + [lax.ppermute(group[s], "x", four(s)) for s in (2, 1, 3)]
    mg = [crossed[i] for i in (0, 2, 1, 3, 4, 6, 5, 7)]
    tok, mg = lax.optimization_barrier((tok, mg))

    stage = pltpu.VMEM((4, 8, 2, 8, 16, SLAB), BF)
    mixed = call(
        mix_kernel, shape(8, 4, 2, 8, 16, SLAB), [wide, swap, stage, pltpu.SemaphoreType.DMA((4,))], n_in=2, hbm=("out",), flops=1 << 30
    )(pos, f1, tok)
    mixed = lax.all_to_all(mixed.reshape(32, 16, 16, SLAB), PLANE, 0, 0, tiled=True).reshape(8, 4, 2, 8, 16, SLAB)
    sent, mgw = call(
        first_apply_kernel, [shape(4, 4, 2, 4, 64, SLAB), shape(COLS, 16 * SLAB)], n_in=9, flops=1 << 30
    )(pos, f1tp, *mg)
    halves = [f32(4, 4, 16, 512)] * 2
    first = call(first_kernel, halves, [wide], n_in=2, flops=1 << 30)(pos, mgw, tok)
    mixed, sent, (first_keep, first_give) = lax.optimization_barrier((mixed, sent, first))

    home = lax.all_to_all(sent.reshape(32, 4, 64, SLAB), ZX, 0, 0, tiled=True)
    second_keep, second_give = call(second_kernel, halves, [wide], n_in=2, flops=1 << 30)(pos, flat, mixed)
    other = [(0, 1), (1, 0)]
    first_came, second_came = lax.ppermute(first_give, "core", other), lax.ppermute(second_give, "core", other)
    sums = call(core_sum_kernel, [f32(4, 2, 16, 512)] * 4, n_in=4)(
        pos, first_keep, first_came, second_keep, second_came
    )
    sums = [sums[0]] + [lax.ppermute(sums[t], "y", four(t)) for t in range(1, 4)]
    sums = call(y_sum_kernel, [f32(2, 16, 512)] * 4, n_in=4, moved=1 << 20)(pos, *sums)
    sums = [sums[0]] + [lax.ppermute(sums[s], "x", four(s)) for s in range(1, 4)]
    sums = call(sum_kernel, f32(2, 16, 512), n_in=4, moved=1 << 19)(pos, *sums)
    sums = lax.ppermute(sums, ("zh", "x"), [(a * 4 + b, b * 4 + a) for a in range(4) for b in range(4)])
    home, first_grad, second_grad = lax.optimization_barrier((home, sums[:1], sums[1:]))
    token_grad = call(
        grad_join_kernel,
        shape(16, 64, 1024),
        [pltpu.VMEM((16, 64, 1024), BF), pltpu.SemaphoreType.DMA((4, 8)), pltpu.SemaphoreType.DMA((4,))],
        hbm=(0, "out"),
    )(pos, home.reshape(4, 4, 2, 4, 64, SLAB))
    return token_grad, first_grad, second_grad


def solution(mesh):
    fine = Mesh(mesh.devices.reshape(4, 4, 2, 4, 2), ("zh", "y", "core", "x", "zl"))
    outer, inner = ("zh", "y", "core"), ("x", "zl")
    grid = P(outer, inner, None)
    factor = P(inner, None, None)
    return jax.shard_map(
        local,
        mesh=fine,
        in_specs=(grid, grid, grid, factor, factor),
        out_specs=(grid, P(inner, outer, None), P(inner, outer, None)),
        check_vma=False,
    )
```

```python
import functools

import jax
import jax.numpy as jnp
from jax import lax
from jax.experimental import pallas as pl
from jax.experimental.pallas import tpu as pltpu
from jax.sharding import Mesh, PartitionSpec as P

ROWS = 512
COLS = 512
SLAB = 128
BF = jnp.bfloat16
F32 = jnp.float32
ZYC = ("zh", "y", "core", "zl")
ZX = ("zh", "x", "zl")
PLANE = ("y", "core", "x")
NEAR, FAR = (0, 1, 7, 2), (6, 3, 5, 4)
PARAMS = pltpu.CompilerParams(vmem_limit_bytes=48 * 1024 * 1024)
VM = pl.BlockSpec(memory_space=pltpu.VMEM)
SM = pl.BlockSpec(memory_space=pltpu.SMEM)
HB = pl.BlockSpec(memory_space=pltpu.HBM)


def call(kernel, outs, scratch=(), n_in=1, hbm=(), flops=0, moved=4 << 20):
    return pl.pallas_call(
        kernel,
        out_shape=outs,
        in_specs=[SM] + [HB if k in hbm else VM for k in range(n_in)],
        out_specs=jax.tree.map(lambda _: HB if "out" in hbm else VM, outs),
        scratch_shapes=list(scratch),
        compiler_params=PARAMS,
        cost_estimate=pl.CostEstimate(flops=flops, bytes_accessed=moved, transcendentals=0),
    )


def shape(*dims, dtype=BF):
    return jax.ShapeDtypeStruct(dims, dtype)


def gate_kernel(gate, up, out, swap):
    for k in range(8):
        lanes = slice(k * SLAB, (k + 1) * SLAB)
        for r in range(16):
            swap[k, pl.ds(r, 16, stride=16), :] = gate[r, :, lanes].astype(F32) * up[r, :, lanes].astype(F32)
        out[k // 2, :, k % 2] = swap[k].astype(BF).reshape(2, 8, 16, SLAB)


def gate_call(gate, up):
    return pl.pallas_call(
        gate_kernel,
        grid=(4,),
        out_shape=shape(4, 8, 2, 8, 16, SLAB),
        in_specs=[pl.BlockSpec((16, 16, 1024), lambda c: (0, c, 0))] * 2,
        out_specs=pl.BlockSpec((4, 2, 2, 8, 16, SLAB), lambda c: (0, c, 0, 0, 0, 0)),
        scratch_shapes=[pltpu.VMEM((8, 256, SLAB), F32)],
        compiler_params=PARAMS,
        cost_estimate=pl.CostEstimate(flops=1 << 20, bytes_accessed=6 << 20, transcendentals=0),
    )(gate, up)


def second_factor_kernel(pos, *refs):
    f2t, full = refs[4:]
    for k in range(4):
        rows = pl.ds(pl.multiple_of((pos[2] ^ k) * 128, 128), 128)
        full[rows, :] = refs[k][0].astype(F32)
    f2t[...] = full[...].T.astype(BF)


def first_factor_kernel(pos, *refs):
    f1, f1tp, full = refs[4:]
    for k in range(4):
        rows = pl.ds(pl.multiple_of((pos[2] ^ k) * 128, 128), 128)
        full[rows, :] = refs[k][0].astype(F32)
    f1[...] = full[...].astype(BF)
    ordered = jnp.concatenate(
        [
            full[x * 128 + zl * 64 + c * 8 : x * 128 + zl * 64 + c * 8 + 8, :]
            for x in range(4)
            for c in range(8)
            for zl in range(2)
        ],
        axis=0,
    )
    f1tp[...] = ordered.T.astype(BF)


def second_apply_kernel(pos, f2t, g, *refs):
    outs, flat, swap = refs[:8], refs[8], refs[9]
    for k in range(16):
        flat[:, k * SLAB : (k + 1) * SLAB] = g[:, :, k // 8, k % 8].reshape(ROWS, SLAB)

    def body(zh, _):
        rows = pl.ds(pl.multiple_of(zh * 128, 128), 128)
        for k in range(0, 16, 2):
            part = jnp.dot(f2t[rows, :], flat[:, k * SLAB : (k + 2) * SLAB], preferred_element_type=F32)
            swap[pl.ds(k, 128, stride=16), :] = part[:, :SLAB]
            swap[pl.ds(k + 1, 128, stride=16), :] = part[:, SLAB:]
        for t, out in enumerate(outs):
            at = pl.multiple_of(lax.rem(pos[3] + t, 8) * 256, 256)
            tile = swap[pl.ds(at, 256), :].astype(BF).reshape(4, 4, 16, SLAB)
            for x in range(4):
                out[x, zh] = tile[x]
        return 0

    lax.fori_loop(0, 4, body, 0)


def second_cut_kernel(pos, a, b, c, d, *outs):
    for s, out in enumerate(outs):
        owner = lax.rem(pos[0] + s, 4)
        for t, block in enumerate((a, b, c, d)):
            out[t] = block[owner]


def first_apply_kernel(pos, f1t, *refs):
    out, mgw = refs[8:]
    for i, steps in enumerate((NEAR, FAR)):
        for s in range(4):
            block = refs[i * 4 + s]
            for j, t in enumerate(steps):
                at = lax.rem(pos[0] + 4 - s, 4) * 128 + lax.rem(pos[3] + 8 - t, 8) * 16
                rows = pl.ds(pl.multiple_of(at, 16), 16)
                for k in range(16):
                    mgw[rows, k * SLAB : (k + 1) * SLAB] = block[j, k // 4, k % 4]
    for k in range(0, 16, 2):
        part = jnp.dot(f1t[...], mgw[:, k * SLAB : (k + 2) * SLAB], preferred_element_type=F32).astype(BF)
        out[k // 4, :, :, k % 4] = part[:, :SLAB].reshape(4, 2, 64, SLAB)
        out[k // 4, :, :, k % 4 + 1] = part[:, SLAB:].reshape(4, 2, 64, SLAB)


def token_cut_kernel(pos, x0, x1, x2, x3, out):
    for s, block in enumerate((x0, x1, x2, x3)):
        source = lax.rem(pos[0] + 4 - s, 4)
        for k in range(8):
            out[k // 2, k % 2, source] = block[:, :, k * SLAB : (k + 1) * SLAB]


def grad_join_kernel(pos, part, out, stage, arrive, leave):
    def into(x, k):
        return pltpu.make_async_copy(
            part.at[k // 2, x, k % 2], stage.at[pl.ds(4 * x, 4), :, pl.ds(SLAB * k, SLAB)], arrive.at[x, k]
        )

    def away(x):
        rows = pl.ds(4 * x, 4)
        return pltpu.make_async_copy(stage.at[rows], out.at[rows], leave.at[x])

    for x in range(4):
        for k in range(8):
            into(x, k).start()
    for x in range(4):
        for k in range(8):
            into(x, k).wait()
        away(x).start()
    for x in range(4):
        away(x).wait()


def mix_kernel(pos, f1, tok, mixed, tokw, swap, stage, sem):
    for k in range(16):
        for x in range(4):
            for zl in range(2):
                at = (x * 2 + zl) * 64
                tokw[at : at + 64, k * SLAB : (k + 1) * SLAB] = tok[k // 4, zl, x, k % 4]

    def copy(b):
        return pltpu.make_async_copy(stage.at[b], mixed.at[:, b], sem.at[b])

    for b in range(4):
        for k in range(0, 16, 2):
            part = jnp.dot(
                f1[b * 128 : (b + 1) * 128, :], tokw[:, k * SLAB : (k + 2) * SLAB], preferred_element_type=F32
            )
            swap[pl.ds(k, 128, stride=16), :] = part[:, :SLAB]
            swap[pl.ds(k + 1, 128, stride=16), :] = part[:, SLAB:]
        for zl in range(2):
            stage[b, :, zl] = swap[zl * 1024 : (zl + 1) * 1024, :].astype(BF).reshape(8, 8, 16, SLAB)
        copy(b).start()
    for b in range(4):
        copy(b).wait()


def first_kernel(pos, mgw, tok, keep, give, tokw):
    for k in range(16):
        for x in range(4):
            for zl in range(2):
                at = (x * 2 + zl) * 64
                tokw[at : at + 64, k * SLAB : (k + 1) * SLAB] = tok[k // 4, zl, x, k % 4]
    for x in range(4):
        left = mgw[x * 128 : (x + 1) * 128, :]
        part = lax.dot_general(left, tokw[...], (((1,), (1,)), ((), ())), preferred_element_type=F32)

        def put(cores):
            for yc in range(8):
                for zl in range(2):
                    at, half = yc * 16 + zl * 8, (yc % 2) * 8
                    cores[(yc // 2) % 2][zl * 2 + yc // 4, x, half : half + 8, :] = part[at : at + 8, :]

        @pl.when(pos[5] == 0)
        def _():
            put((keep, give))

        @pl.when(pos[5] == 1)
        def _():
            put((give, keep))


def second_kernel(pos, flat, mixed, keep, give, mixw):
    core = pos[5]
    for k in range(16):
        lanes = slice(k * SLAB, (k + 1) * SLAB)
        mixw[:, lanes] = mixed[:, :, k // 8, k % 8].reshape(ROWS, SLAB)
    for zh in range(4):
        part = lax.dot_general(
            flat[zh * 128 : (zh + 1) * 128, :], mixw[...], (((1,), (1,)), ((), ())), preferred_element_type=F32
        )

        def put(keep, give):
            for y in range(4):
                keep[y, zh] = part[y * 32 : y * 32 + 16, :]
                give[y, zh] = part[y * 32 + 16 : y * 32 + 32, :]

        @pl.when(core == 0)
        def _():
            put(keep, give)

        @pl.when(core == 1)
        def _():
            put(give, keep)


def core_sum_kernel(pos, f, fo, s, so, *outs):
    for t, out in enumerate(outs):
        y = lax.rem(pos[4] + t, 4)
        out[:, 0] = f[y] + fo[y]
        out[:, 1] = s[y] + so[y]


def y_sum_kernel(pos, a, b, c, d, *outs):
    for s, out in enumerate(outs):
        x = lax.rem(pos[0] + s, 4)
        out[...] = (a[x] + b[x]) + (c[x] + d[x])


def sum_kernel(pos, a, b, c, d, out):
    place = lax.broadcasted_iota(jnp.int32, (ROWS, ROWS), 0)
    row = lax.broadcasted_iota(jnp.int32, (ROWS, ROWS), 1)
    want = ((row >> 4) & 7) * 64 + ((row >> 2) & 3) * 16 + (row >> 7) * 4 + (row & 3)
    order = (place == want).astype(F32)
    out[0] = ((a[0] + b[0]) + (c[0] + d[0])) * (ROWS**-0.5 * SLAB**-0.5)
    total = (a[1] + b[1]) + (c[1] + d[1])
    second = jnp.dot(total, order, precision=lax.Precision.HIGHEST, preferred_element_type=F32)
    out[1] = second * (COLS**-0.5 * SLAB**-0.5)


def shifts(count):
    return lambda s: [(k, (k + s) % count) for k in range(count)]


def local(tokens, gate, upstream, first_factor, second_factor):
    zh, zl = lax.axis_index("zh"), lax.axis_index("zl")
    x, y, core = lax.axis_index("x"), lax.axis_index("y"), lax.axis_index("core")
    z, yc, part = zh * 2 + zl, y * 2 + core, (y % 2) * 2 + core
    pos = jnp.stack([x, z, part, yc, y, core]).astype(jnp.int32)
    four, eight = shifts(4), shifts(8)
    wide = pltpu.VMEM((ROWS, 16 * SLAB), BF)
    swap = pltpu.VMEM((128 * 16, SLAB), F32)
    f32 = functools.partial(shape, dtype=F32)

    gated = gate_call(gate, upstream)
    grad = lax.all_to_all(gated.reshape(64, 8, 16, SLAB), ZYC, 0, 0, tiled=True).reshape(4, 8, 2, 8, 16, SLAB)
    tok_x = []
    for s in range(4):
        piece = lax.dynamic_slice_in_dim(tokens, ((x + s) % 4) * 4, 4, 0)
        tok_x.append(piece if s == 0 else lax.ppermute(piece, "x", four(s)))
    sent = call(token_cut_kernel, shape(4, 2, 4, 4, 64, SLAB), n_in=4)(pos, *tok_x)

    both = jnp.concatenate([first_factor, second_factor], 0)
    quarter = lax.dynamic_slice_in_dim(both, part * 128, 128, 1)
    got = quarter
    for s in range(1, 4):
        came = lax.ppermute(quarter, ("zh", "x"), [(k * 4 + k, k * 4 + (k + s) % 4) for k in range(4)])
        got = jnp.where(x == (zh + s) % 4, came, got)

    def gathered(own):
        return [own] + [lax.ppermute(own, ("y", "core"), [(k, k ^ s) for k in range(8)]) for s in range(1, 4)]

    full = pltpu.VMEM((COLS, COLS), F32)
    f2t = call(second_factor_kernel, shape(ROWS, ROWS), [full], n_in=4, moved=1 << 20)(pos, *gathered(got[1:]))
    first_quarters = gathered(got[:1])
    first_quarters, sent, grad, f2t = lax.optimization_barrier((first_quarters, sent, grad, f2t))

    tok = lax.all_to_all(sent.reshape(8, 16, 64, SLAB), ("zh", "zl"), 0, 0, tiled=True).reshape(4, 2, 4, 4, 64, SLAB)
    f1, f1tp = call(first_factor_kernel, [shape(COLS, COLS)] * 2, [full], n_in=4, moved=1 << 20)(
        pos, *first_quarters
    )
    *mg, flat = call(
        second_apply_kernel,
        [shape(4, 4, 4, 16, SLAB)] * 8 + [shape(ROWS, 16 * SLAB)],
        [swap],
        n_in=2,
        flops=1 << 30,
    )(pos, f2t, grad)
    crossed = []
    for steps in (NEAR, FAR):
        group = [mg[t] if t == 0 else lax.ppermute(mg[t], ("y", "core"), eight(t)) for t in steps]
        group = call(second_cut_kernel, [shape(4, 4, 4, 16, SLAB)] * 4, n_in=4, moved=1 << 21)(pos, *group)
        crossed += [group[0]] + [lax.ppermute(group[s], "x", four(s)) for s in (2, 1, 3)]
    mg = [crossed[i] for i in (0, 2, 1, 3, 4, 6, 5, 7)]
    tok, mg = lax.optimization_barrier((tok, mg))

    stage = pltpu.VMEM((4, 8, 2, 8, 16, SLAB), BF)
    mixed = call(
        mix_kernel, pltpu.HBM((8, 4, 2, 8, 16, SLAB), BF), [wide, swap, stage, pltpu.SemaphoreType.DMA((4,))], n_in=2, hbm=("out",), flops=1 << 30
    )(pos, f1, tok)
    mixed = lax.all_to_all(mixed.reshape(32, 16, 16, SLAB), PLANE, 0, 0, tiled=True).reshape(8, 4, 2, 8, 16, SLAB)
    sent, mgw = call(
        first_apply_kernel, [shape(4, 4, 2, 4, 64, SLAB), shape(COLS, 16 * SLAB)], n_in=9, flops=1 << 30
    )(pos, f1tp, *mg)
    halves = [f32(4, 4, 16, 512)] * 2
    first = call(first_kernel, halves, [wide], n_in=2, flops=1 << 30)(pos, mgw, tok)
    mixed, sent, (first_keep, first_give) = lax.optimization_barrier((mixed, sent, first))

    home = lax.all_to_all(sent.reshape(32, 4, 64, SLAB), ZX, 0, 0, tiled=True)
    second_keep, second_give = call(second_kernel, halves, [wide], n_in=2, flops=1 << 30)(pos, flat, mixed)
    other = [(0, 1), (1, 0)]
    first_came, second_came = lax.ppermute(first_give, "core", other), lax.ppermute(second_give, "core", other)
    sums = call(core_sum_kernel, [f32(4, 2, 16, 512)] * 4, n_in=4)(
        pos, first_keep, first_came, second_keep, second_came
    )
    sums = [sums[0]] + [lax.ppermute(sums[t], "y", four(t)) for t in range(1, 4)]
    sums = call(y_sum_kernel, [f32(2, 16, 512)] * 4, n_in=4, moved=1 << 20)(pos, *sums)
    sums = [sums[0]] + [lax.ppermute(sums[s], "x", four(s)) for s in range(1, 4)]
    sums = call(sum_kernel, f32(2, 16, 512), n_in=4, moved=1 << 19)(pos, *sums)
    sums = lax.ppermute(sums, ("zh", "x"), [(a * 4 + b, b * 4 + a) for a in range(4) for b in range(4)])
    home, first_grad, second_grad = lax.optimization_barrier((home, sums[:1], sums[1:]))
    token_grad = call(
        grad_join_kernel,
        shape(16, 64, 1024),
        [pltpu.VMEM((16, 64, 1024), BF), pltpu.SemaphoreType.DMA((4, 8)), pltpu.SemaphoreType.DMA((4,))],
        hbm=(0, "out"),
    )(pos, home.reshape(4, 4, 2, 4, 64, SLAB))
    return token_grad, first_grad, second_grad


def solution(mesh):
    fine = Mesh(mesh.devices.reshape(4, 4, 2, 4, 2), ("zh", "y", "core", "x", "zl"))
    outer, inner = ("zh", "y", "core"), ("x", "zl")
    grid = P(outer, inner, None)
    factor = P(inner, None, None)
    return jax.shard_map(
        local,
        mesh=fine,
        in_specs=(grid, grid, grid, factor, factor),
        out_specs=(grid, P(inner, outer, None), P(inner, outer, None)),
        check_vma=False,
    )
```
